256 devices in a mesh: grp: 16 (over z, y_lo), tp: 16 (over y_hi, x, core).
Axes of the slice: x: 4, y: 4 (y_hi: 2, y_lo: 2; y = y_hi * 2 + y_lo), z: 8, core: 2. Of those that a mesh axis runs over, the one named last changes fastest.
Arguments:
- activations: bfloat16 [98304, 8192], P('grp', 'tp'), may hold values from -6 to 6
- cotangents: bfloat16 [98304, 8192], P('grp', 'tp'), may hold values from -6 to 6
- adapter_down_weight: bfloat16 [8192, 16], P('tp'), may hold values from -0.0625 to 0.0625
- adapter_up_weight: bfloat16 [16, 8192], P(None, 'tp'), may hold values from -1.5 to 1.5
- sign_flag_bits: int32 [8192, 256], P('tp'), may hold values from 0 to 1
- validation_feature_rows: float32 [512, 8192], P('grp', 'tp'), may hold values from -6 to 6
Outputs:
- scores: float32 [96, 512], P('grp', 'tp')
The draws below stay inside these ranges and needn't reach their ends.
All inputs are finite; a program needn't handle non-finite values.
Results may differ from the reference program's by a relative error of at most 0.0003.
Values sent between devices are 32-bit elements; how exact they have to be, the bound alone decides.
No kernel may reach another device: no remote copies, remote signals or barrier semaphores. Data moves between devices by JAX's collectives and lax.ppermute only.
A program may use at most 128 MiB of HBM per device.

```python
import math
import jax
import jax.numpy as jnp
from jax import lax

MODEL_WIDTH = 8192
ADAPTER_RANK = 16
KD = 256
LEN = 1024
NVAL = 512
K = 8192
TOKENS = 98304


def place_ends(values, own_key, least, largest):
    longest = values.shape.index(max(values.shape))
    spots = []
    for shift in (0, 1):
        where = [jax.random.randint(jax.random.fold_in(own_key, axis), (), 0, length) for axis, length in enumerate(values.shape)]
        where[longest] = (where[longest] + shift) % values.shape[longest]
        spots.append(tuple(where))
    return values.at[spots[0]].set(least).at[spots[1]].set(largest)


def steps_of(stream_key, shape, cuts, low, top_value):
    loudness, own = 1.0, jax.random.fold_in(stream_key, 6)
    for dim, parts in cuts:
        heights = jnp.exp(jax.random.uniform(jax.random.fold_in(own, dim), (parts,), jnp.float32, low / len(cuts), top_value / len(cuts)))
        loudness = loudness * jnp.repeat(heights, shape[dim] // parts).reshape([-1 if axis == dim else 1 for axis in range(len(shape))])
    return loudness


def noise(stream_key, dims, deviation, reach, cuts=(), kind=jnp.bfloat16):
    entries = deviation * jax.random.normal(stream_key, dims, jnp.float32)
    if cuts:
        entries = entries * steps_of(stream_key, dims, cuts, -0.22, 0.18)
    return jnp.clip(entries, -reach, reach).astype(kind)


def setup_inputs(seed: int = 0) -> dict:
    key_of = jax.random.split(jax.random.key(seed), 7)
    activations = noise(key_of[0], (TOKENS, MODEL_WIDTH), 1.0, 6.0, ((0, 16), (1, 16)))
    cotangents = noise(key_of[1], (TOKENS, MODEL_WIDTH), 1.0, 6.0, ((0, 16), (1, 16)))
    adapter_down_weight = noise(key_of[2], (MODEL_WIDTH, ADAPTER_RANK), MODEL_WIDTH ** -0.5, 0.0625, ((0, 16),))
    adapter_up_weight = noise(key_of[3], (ADAPTER_RANK, MODEL_WIDTH), ADAPTER_RANK ** -0.5, 1.5, ((1, 16),))
    sign_flag_bits = place_ends(jax.random.randint(key_of[4], (MODEL_WIDTH, KD), 0, 2), jax.random.fold_in(key_of[4], 1), 0, 1).astype(jnp.int32)
    validation_feature_rows = noise(key_of[5], (NVAL, K), 1.0, 6.0, ((0, 16), (1, 16)), jnp.float32)
    return dict(activations=activations, cotangents=cotangents, adapter_down_weight=adapter_down_weight, adapter_up_weight=adapter_up_weight, sign_flag_bits=sign_flag_bits, validation_feature_rows=validation_feature_rows)


def reference(activations, cotangents, adapter_down_weight, adapter_up_weight, sign_flag_bits, validation_feature_rows):
    sign_projector = (2 * sign_flag_bits - 1).astype(jnp.bfloat16)
    proj_x = jnp.dot(activations, sign_projector, preferred_element_type=jnp.float32)
    proj_g = jnp.dot(cotangents, sign_projector, preferred_element_type=jnp.float32)
    down_activation = jnp.dot(activations, adapter_down_weight, preferred_element_type=jnp.float32)
    up_gradient = jnp.dot(cotangents, jnp.transpose(adapter_up_weight), preferred_element_type=jnp.float32)
    seq_total = activations.shape[0] // LEN
    grad_a = jnp.einsum('slk,slr->skr', proj_x.reshape(seq_total, LEN, KD), up_gradient.reshape(seq_total, LEN, ADAPTER_RANK), precision=lax.Precision.HIGHEST)
    grad_b = jnp.einsum('slk,slr->skr', proj_g.reshape(seq_total, LEN, KD), down_activation.reshape(seq_total, LEN, ADAPTER_RANK), precision=lax.Precision.HIGHEST)
    features = jnp.stack([grad_a, grad_b], 1).reshape(seq_total, K)
    train_sq = lax.optimization_barrier(jnp.sum(features * features, axis=1))
    valid_sq = lax.optimization_barrier(jnp.sum(validation_feature_rows * validation_feature_rows, axis=1))
    unit_train = features * (math.sqrt(K) / jnp.sqrt(train_sq + 1e-06))[:, None]
    unit_valid = validation_feature_rows / jnp.sqrt(valid_sq + 1e-06)[:, None]
    return jnp.dot(unit_train, jnp.transpose(unit_valid), precision=lax.Precision.HIGHEST)
```

```python
import functools
import math

import jax
import jax.numpy as jnp
from jax import lax
from jax.experimental import pallas as pl
from jax.experimental.pallas import tpu as pltpu
from jax.sharding import PartitionSpec as P

LEN = 1024
K = 8192
TB = 512
EPS = 1e-06
VMEM = 48 * 1024 * 1024

NT = (((1,), (1,)), ((), ()))
NN = (((1,), (0,)), ((), ()))


def mm(a, b, dims):
    return lax.dot_general(a, b, dims, preferred_element_type=jnp.float32)


def halves(a):
    hi = a.astype(jnp.bfloat16)
    lo = (a - hi.astype(jnp.float32)).astype(jnp.bfloat16)
    return jnp.concatenate([hi, lo], 0)


def rows_kernel(core_ref, x_ref, g_ref, a_ref, b_ref, keep_ref, send_ref, at_ref):
    @pl.when(pl.program_id(0) == 0)
    def _():
        at_ref[...] = jnp.transpose(a_ref[...].astype(jnp.float32)).astype(jnp.bfloat16)

    down = mm(at_ref[...], x_ref[...], NT)
    up = mm(b_ref[...], g_ref[...], NT)
    first = core_ref[0] == 0
    keep_ref[0] = jnp.where(first, down, up)
    send_ref[0] = jnp.where(first, up, down)


def rank_rows(core, x, g, a, b):
    tokens, width = x.shape
    rank = b.shape[0]
    chunk = tokens // 4
    per = chunk // TB
    out = jax.ShapeDtypeStruct((4, rank, chunk), jnp.float32)
    out_spec = pl.BlockSpec((1, rank, TB), lambda i: (i // per, 0, i % per))
    return pl.pallas_call(
        rows_kernel,
        grid=(tokens // TB,),
        in_specs=[
            pl.BlockSpec(memory_space=pltpu.SMEM),
            pl.BlockSpec((TB, width), lambda i: (i, 0)),
            pl.BlockSpec((TB, width), lambda i: (i, 0)),
            pl.BlockSpec((width, rank), lambda i: (0, 0)),
            pl.BlockSpec((rank, width), lambda i: (0, 0)),
        ],
        out_specs=[out_spec, out_spec],
        out_shape=[out, out],
        scratch_shapes=[pltpu.VMEM((rank, width), jnp.bfloat16)],
        compiler_params=pltpu.CompilerParams(vmem_limit_bytes=VMEM),
        cost_estimate=pl.CostEstimate(
            flops=4 * tokens * width * rank, bytes_accessed=4 * tokens * width, transcendentals=0
        ),
        name="rank_rows",
    )(core, x, g, a, b)


def share_kernel(core_ref, x_ref, g_ref, own_ref, other_ref, s_ref, out_ref, v_ref):
    i = pl.program_id(0)
    rank = own_ref.shape[1]
    first = core_ref[0] == 0
    own, other = own_ref[0], other_ref[0]
    up = halves(jnp.where(first, other, own))
    down = halves(jnp.where(first, own, other))
    va = mm(up, x_ref[...], NN)
    vb = mm(down, g_ref[...], NN)
    va = va[:rank] + va[rank:]
    vb = vb[:rank] + vb[rank:]
    here = pl.ds(pl.multiple_of((i * TB // LEN) * rank, rank), rank)

    @pl.when(i == 0)
    def _():
        v_ref[...] = jnp.zeros_like(v_ref)

    v_ref[0, here, :] += va
    v_ref[1, here, :] += vb

    @pl.when(i == pl.num_programs(0) - 1)
    def _():
        sign = (2 * s_ref[...] - 1).astype(jnp.float32).astype(jnp.bfloat16)
        each = out_ref.shape[0] // 2
        for m in range(2):
            f = mm(halves(v_ref[m]), sign, NN)
            f = jnp.transpose(f[:128] + f[128:])
            out_ref[m * each : (m + 1) * each] = f.reshape(each, -1, 128)


def feature_shares(core, x, g, own, other, bits, parts):
    tokens, width = x.shape
    rank, chunk = own.shape[1:]
    per = chunk // TB
    kd = bits.shape[1]
    row_spec = pl.BlockSpec((1, rank, TB), lambda i: (i // per, 0, i % per))
    return pl.pallas_call(
        share_kernel,
        grid=(tokens // TB,),
        in_specs=[
            pl.BlockSpec(memory_space=pltpu.SMEM),
            pl.BlockSpec((TB, width), lambda i: (i, 0)),
            pl.BlockSpec((TB, width), lambda i: (i, 0)),
            row_spec,
            row_spec,
            pl.BlockSpec((width, kd), lambda i: (0, 0)),
        ],
        out_specs=pl.BlockSpec((parts, 2 * kd // parts, 128), lambda i: (0, 0, 0)),
        out_shape=jax.ShapeDtypeStruct((parts, 2 * kd // parts, 128), jnp.float32),
        scratch_shapes=[pltpu.VMEM((2, 128, width), jnp.float32)],
        compiler_params=pltpu.CompilerParams(vmem_limit_bytes=VMEM),
        cost_estimate=pl.CostEstimate(
            flops=8 * tokens * width * rank, bytes_accessed=4 * tokens * width, transcendentals=0
        ),
        name="feature_shares",
    )(core, x, g, own, other, bits)


def valid_kernel(rank, v_ref, hl_ref, sq_ref):
    v = v_ref[...]
    rows, cols = v.shape
    ks = cols // rank
    came = lax.broadcasted_iota(jnp.int32, (cols, cols), 0)
    goes = lax.broadcasted_iota(jnp.int32, (cols, cols), 1)
    move = jnp.where((came % rank) * ks + came // rank == goes, 1.0, 0.0).astype(jnp.bfloat16)
    hl_ref[...] = mm(halves(v), move, NN).astype(jnp.bfloat16)
    sq = halves(v * v)
    total = mm(jnp.ones((8, cols), jnp.bfloat16), sq, NT)
    sq_ref[...] = total[:, :rows] + total[:, rows:]


def valid_terms(v, rank):
    rows, cols = v.shape
    return pl.pallas_call(
        functools.partial(valid_kernel, rank),
        out_shape=[
            jax.ShapeDtypeStruct((2 * rows, cols), jnp.bfloat16),
            jax.ShapeDtypeStruct((8, rows), jnp.float32),
        ],
        compiler_params=pltpu.CompilerParams(vmem_limit_bytes=VMEM),
        cost_estimate=pl.CostEstimate(
            flops=4 * rows * cols * cols, bytes_accessed=8 * rows * cols, transcendentals=0
        ),
        name="valid_terms",
    )(v)


def dot_kernel(rank, f_ref, hl_ref, sq_ref, out_ref, t_ref):
    parts = f_ref.shape[0]
    rows = sq_ref.shape[1]
    each = rows // parts
    t_ref[...] = jnp.transpose(jnp.sum(f_ref[...], 0))
    f = jnp.concatenate([t_ref[pl.ds(r, 8, stride=rank), :] for r in range(rank)], 1)
    prod = mm(halves(f), hl_ref[...], NT)
    dots = prod[:8, :rows] + (prod[8:, :rows] + prod[:8, rows:]) + prod[8:, rows:]
    line = lax.broadcasted_iota(jnp.int32, dots.shape, 0)
    dots = jnp.where(line == 6, sq_ref[...], dots)
    own_sq = jnp.broadcast_to(jnp.sum(f * f, 1, keepdims=True), (8, each))
    for part in range(parts):
        out_ref[part, :, :each] = dots[:, part * each : (part + 1) * each]
        out_ref[part, :, each : 2 * each] = own_sq


def partial_dots(f, hl, sq, rank):
    return pl.pallas_call(
        functools.partial(dot_kernel, rank),
        out_shape=jax.ShapeDtypeStruct((f.shape[0], 8, 128), jnp.float32),
        scratch_shapes=[pltpu.VMEM((128, f.shape[1]), jnp.float32)],
        compiler_params=pltpu.CompilerParams(vmem_limit_bytes=VMEM),
        name="partial_dots",
    )(f, hl, sq)


def score_kernel(p_ref, out_ref):
    seqs, each = out_ref.shape
    p = jnp.sum(p_ref[...], 0)
    train = math.sqrt(K) / jnp.sqrt(p[:seqs, each : 2 * each] + EPS)
    valid = jnp.sqrt(p[6:7, :each] + EPS)
    out_ref[...] = p[:seqs, :each] * train / valid


def on_device(x, g, a, b, bits, valid):
    tp = lax.axis_size("tp")
    grp = lax.axis_size("grp")
    rank = b.shape[0]
    seqs = x.shape[0] // LEN
    core = (lax.axis_index("tp") % 2).astype(jnp.int32).reshape(1)
    swap_core = [(i, i ^ 1) for i in range(tp)]
    swap_y = [(i, i ^ 8) for i in range(tp)]
    along_x = [[(y << 3) | (q << 1) | c for q in range(4)] for y in range(2) for c in range(2)]

    everyone = jnp.broadcast_to(valid[None], (grp, *valid.shape))
    gathered = lax.all_to_all(everyone, "grp", 0, 0, tiled=True).reshape(-1, valid.shape[1])

    keep, send = rank_rows(core, x, g, a, b)
    mine = keep + lax.ppermute(send, "tp", swap_core)
    mine = lax.all_to_all(mine, "tp", 0, 0, axis_index_groups=along_x, tiled=True)
    mine = jnp.sum(mine, 0)
    mine = mine + lax.ppermute(mine, "tp", swap_y)
    mine = jnp.broadcast_to(mine[None], (4, *mine.shape))
    mine = lax.all_to_all(mine, "tp", 0, 0, axis_index_groups=along_x, tiled=True)
    other = lax.ppermute(mine, "tp", swap_core)

    hl, sq = valid_terms(gathered, rank)
    shares = feature_shares(core, x, g, mine, other, bits, tp)
    shares = lax.all_to_all(shares, "tp", 0, 0, tiled=True)
    dots = partial_dots(shares, hl, sq, rank)
    dots = lax.all_to_all(dots, "tp", 0, 0, tiled=True)
    return pl.pallas_call(
        score_kernel,
        out_shape=jax.ShapeDtypeStruct((seqs, grp * valid.shape[0] // tp), jnp.float32),
        name="scores",
    )(dots)


def solution(mesh):
    return jax.shard_map(
        on_device,
        mesh=mesh,
        in_specs=(
            P("grp", "tp"),
            P("grp", "tp"),
            P("tp", None),
            P(None, "tp"),
            P("tp", None),
            P("grp", "tp"),
        ),
        out_specs=P("grp", "tp"),
        check_vma=False,
    )
```

```python
import functools
import math

import jax
import jax.numpy as jnp
from jax import lax
from jax.experimental import pallas as pl
from jax.experimental.pallas import tpu as pltpu
from jax.sharding import PartitionSpec as P

LEN = 1024
K = 8192
TB = 512
EPS = 1e-06
VMEM = 20 * 1024 * 1024
STEPS = (2, 2, 2, 2, 2, 1, 1)

NT = (((1,), (1,)), ((), ()))
NN = (((1,), (0,)), ((), ()))


def mm(a, b, dims):
    return lax.dot_general(a, b, dims, preferred_element_type=jnp.float32)


def halves(a):
    hi = a.astype(jnp.bfloat16)
    lo = (a - hi.astype(jnp.float32)).astype(jnp.bfloat16)
    return jnp.concatenate([hi, lo], 0)


def rows_kernel(steps, where_ref, x_ref, g_ref, a_ref, b_ref, keep_ref, send_ref, xs_ref, gs_ref, at_ref, bs_ref, sem, sem_w):
    first = where_ref[0] == 0
    per = keep_ref.shape[2] // TB
    weights = [
        pltpu.make_async_copy(src, dst, sem_w.at[j])
        for j, (src, dst) in enumerate(((a_ref, at_ref), (b_ref, bs_ref)))
    ]
    for copy in weights:
        copy.start()
    copies, start = [], 0
    for c, blocks in enumerate(steps):
        rows = pl.ds(start * TB, blocks * TB)
        pair = [
            pltpu.make_async_copy(src.at[rows], dst.at[rows], sem.at[j, c])
            for j, (src, dst) in enumerate(((x_ref, xs_ref), (g_ref, gs_ref)))
        ]
        for copy in pair:
            copy.start()
        copies.append((start, blocks, pair))
        start += blocks
    for copy in weights:
        copy.wait()
    for start, blocks, pair in copies:
        for copy in pair:
            copy.wait()
        for i in range(start, start + blocks):
            rows = slice(i * TB, (i + 1) * TB)
            cols = slice(i % per * TB, (i % per + 1) * TB)
            down = mm(at_ref[...], xs_ref[rows], NT)
            up = mm(bs_ref[...], gs_ref[rows], NT)
            slot = (i // per - where_ref[2]) & 3
            keep_ref[slot, :, cols] = jnp.where(first, down, up)
            send_ref[slot, :, cols] = jnp.where(first, up, down)


def rank_rows(where, x, g, a, b):
    tokens, width = x.shape
    rank = b.shape[0]
    chunk = tokens // 4
    steps = STEPS
    out = jax.ShapeDtypeStruct((4, rank, chunk), jnp.float32)
    near = pltpu.VMEM((tokens, width), jnp.bfloat16)
    whole = pl.BlockSpec(memory_space=pltpu.VMEM)
    far = pl.BlockSpec(memory_space=pl.ANY)
    x, g, a, b = (pltpu.with_memory_space_constraint(v, pltpu.HBM) for v in (x, g, a, b))
    return pl.pallas_call(
        functools.partial(rows_kernel, steps),
        in_specs=[pl.BlockSpec(memory_space=pltpu.SMEM), far, far, far, far],
        out_specs=[whole] * 4,
        out_shape=[out, out, near, near],
        scratch_shapes=[
            pltpu.VMEM((rank, width), jnp.bfloat16),
            pltpu.VMEM((rank, width), jnp.bfloat16),
            pltpu.SemaphoreType.DMA((2, len(steps))),
            pltpu.SemaphoreType.DMA((2,)),
        ],
        compiler_params=pltpu.CompilerParams(vmem_limit_bytes=VMEM),
        cost_estimate=pl.CostEstimate(
            flops=4 * tokens * width * rank, bytes_accessed=4 * tokens * width, transcendentals=0
        ),
        name="rank_rows",
    )(where, x, g, a, b)


def share_kernel(where_ref, x_ref, g_ref, *refs):
    own_refs, (other_ref, s_ref, out_ref, v_ref) = refs[:4], refs[4:]
    rank, chunk = own_refs[0].shape
    per = chunk // TB
    first = where_ref[0] == 0
    for j, own_ref in enumerate(own_refs):
        begin = ((where_ref[2] - j) & 3) * per
        for c in range(per):
            rows = pl.ds(pl.multiple_of((begin + c) * TB, TB), TB)
            cols = slice(c * TB, (c + 1) * TB)
            own, other = own_ref[:, cols], other_ref[j, :, cols]
            a = mm(halves(jnp.where(first, other, own)), x_ref[rows], NN)
            b = mm(halves(jnp.where(first, own, other)), g_ref[rows], NN)
            v_ref[0, begin + c] = a[:rank] + a[rank:]
            v_ref[1, begin + c] = b[:rank] + b[rank:]
    sign = (2 * s_ref[...] - 1).astype(jnp.float32).astype(jnp.bfloat16)
    each = out_ref.shape[0] // 2
    blocks, step = v_ref.shape[1], LEN // TB
    pad = jnp.zeros((128 - blocks // step * rank, x_ref.shape[1]), jnp.float32)
    for m in range(2):
        v = [sum(v_ref[m, i + k] for k in range(step)) for i in range(0, blocks, step)]
        f = mm(halves(jnp.concatenate(v + [pad], 0)), sign, NN)
        f = jnp.transpose(f[:128] + f[128:])
        out_ref[m * each : (m + 1) * each] = f.reshape(each, -1, 128)


def feature_shares(where, x, g, own, other, bits, parts):
    tokens, width = x.shape
    rank = own[0].shape[0]
    kd = bits.shape[1]
    whole = pl.BlockSpec(memory_space=pltpu.VMEM)
    x, g = (pltpu.with_memory_space_constraint(v, pltpu.VMEM) for v in (x, g))
    return pl.pallas_call(
        share_kernel,
        in_specs=[pl.BlockSpec(memory_space=pltpu.SMEM)] + [whole] * (len(own) + 4),
        out_specs=whole,
        out_shape=jax.ShapeDtypeStruct((parts, 2 * kd // parts, 128), jnp.float32),
        scratch_shapes=[pltpu.VMEM((2, tokens // TB, rank, width), jnp.float32)],
        compiler_params=pltpu.CompilerParams(vmem_limit_bytes=VMEM),
        cost_estimate=pl.CostEstimate(
            flops=8 * tokens * width * rank, bytes_accessed=4 * tokens * width, transcendentals=0
        ),
        name="feature_shares",
    )(where, x, g, *own, other, bits)


def valid_kernel(rank, near_ref, far_ref, hl_ref, sq_ref):
    v = jnp.concatenate([near_ref[...], far_ref[...]], 0)
    rows, cols = v.shape
    ks = cols // rank
    came = lax.broadcasted_iota(jnp.int32, (cols, cols), 0)
    goes = lax.broadcasted_iota(jnp.int32, (cols, cols), 1)
    move = jnp.where((came % rank) * ks + came // rank == goes, 1.0, 0.0).astype(jnp.bfloat16)
    hl_ref[...] = mm(halves(v), move, NN).astype(jnp.bfloat16)
    sq = halves(v * v)
    total = mm(jnp.ones((8, cols), jnp.bfloat16), sq, NT)
    sq_ref[...] = total[:, :rows] + total[:, rows:]


def valid_terms(near, far, rank):
    rows, cols = 2 * near.shape[0], near.shape[1]
    return pl.pallas_call(
        functools.partial(valid_kernel, rank),
        out_shape=[
            jax.ShapeDtypeStruct((2 * rows, cols), jnp.bfloat16),
            jax.ShapeDtypeStruct((8, rows), jnp.float32),
        ],
        compiler_params=pltpu.CompilerParams(vmem_limit_bytes=VMEM),
        cost_estimate=pl.CostEstimate(
            flops=4 * rows * cols * cols, bytes_accessed=8 * rows * cols, transcendentals=0
        ),
        name="valid_terms",
    )(near, far)


def flip(step, z, y):
    if step == 0:
        return z ^ 4, y
    if step == 1:
        return z ^ 1, y
    if step == 2:
        return z, y ^ 1
    return (z + 2 * (z & 1) - 1) & 7, y


def flips(step):
    pairs = []
    for i in range(16):
        z, y = flip(step, i >> 1, i & 1)
        pairs.append((i, z * 2 + y))
    return pairs


def origin(place, index):
    z, y = index >> 1, index & 1
    for step in (3, 2, 1, 0):
        if place >> step & 1:
            z, y = flip(step, z, y)
    return z * 2 + y


def dot_kernel(rank, where_ref, f_ref, hl_ref, sq_ref, out_ref, t_ref):
    parts = f_ref.shape[0]
    rows = sq_ref.shape[1]
    each = rows // parts
    t_ref[...] = jnp.transpose(jnp.sum(f_ref[...], 0))
    f = jnp.concatenate([t_ref[pl.ds(r, 8, stride=rank), :] for r in range(rank)], 1)
    prod = mm(halves(f), hl_ref[...], NT)
    dots = prod[:8, :rows] + (prod[8:, :rows] + prod[:8, rows:]) + prod[8:, rows:]
    line = lax.broadcasted_iota(jnp.int32, dots.shape, 0)
    dots = jnp.where(line == 6, sq_ref[...], dots)
    own_sq = jnp.broadcast_to(jnp.sum(f * f, 1, keepdims=True), (8, each))
    for place in range(parts):
        part = origin(place, where_ref[1])
        out_ref[part, :, :each] = dots[:, place * each : (place + 1) * each]
        out_ref[part, :, each : 2 * each] = own_sq


def partial_dots(where, f, hl, sq, rank):
    whole = pl.BlockSpec(memory_space=pltpu.VMEM)
    return pl.pallas_call(
        functools.partial(dot_kernel, rank),
        in_specs=[pl.BlockSpec(memory_space=pltpu.SMEM), whole, whole, whole],
        out_shape=jax.ShapeDtypeStruct((f.shape[0], 8, 128), jnp.float32),
        scratch_shapes=[pltpu.VMEM((128, f.shape[1]), jnp.float32)],
        compiler_params=pltpu.CompilerParams(vmem_limit_bytes=VMEM),
        name="partial_dots",
    )(where, f, hl, sq)


def on_device(x, g, a, b, bits, valid):
    tp = lax.axis_size("tp")
    rank = b.shape[0]
    seqs = x.shape[0] // LEN
    each = 16 * valid.shape[0] // tp
    index = lax.axis_index("tp")
    where = jnp.stack([index & 1, lax.axis_index("grp"), index >> 1 & 3]).astype(jnp.int32)
    swap_core = [(i, i ^ 1) for i in range(tp)]
    swap_y = [(i, i ^ 8) for i in range(tp)]
    turn_x = [[(i, (i & 9) | (((i >> 1) + k & 3) << 1)) for i in range(tp)] for k in range(4)]

    def gather(step, rows, after):
        rows, after = lax.optimization_barrier((rows, after))
        return rows, lax.ppermute(rows, "grp", flips(step)), after

    keep, send, x, g = rank_rows(where, x, g, jnp.transpose(a), b)
    near, far, send = gather(0, valid, send)
    mine = keep + lax.ppermute(send, "tp", swap_core)
    came = [lax.ppermute(mine[k], "tp", turn_x[k]) for k in (1, 2, 3)]
    mine = mine[0] + came[0] + came[1] + came[2]
    near, far, mine = gather(1, jnp.concatenate([near, far], 0), mine)
    mine = mine + lax.ppermute(mine, "tp", swap_y)
    near, far, mine = gather(2, jnp.concatenate([near, far], 0), mine)
    own = [mine] + [lax.ppermute(mine, "tp", turn_x[k]) for k in (1, 2, 3)]
    near, far, own = gather(3, jnp.concatenate([near, far], 0), own)
    other = lax.ppermute(jnp.stack(own), "tp", swap_core)

    shares = feature_shares(where, x, g, own, other, bits, tp)
    hl, sq = valid_terms(near, far, rank)
    shares = lax.all_to_all(shares, "tp", 0, 0, tiled=True)
    dots = partial_dots(where, shares, hl, sq, rank)
    dots = lax.all_to_all(dots, "tp", 0, 0, tiled=True)
    total = jnp.sum(dots, 0)
    train = math.sqrt(K) / jnp.sqrt(total[:seqs, each : 2 * each] + EPS)
    return total[:seqs, :each] * train / jnp.sqrt(total[6:7, :each] + EPS)


def solution(mesh):
    return jax.shard_map(
        on_device,
        mesh=mesh,
        in_specs=(
            P("grp", "tp"),
            P("grp", "tp"),
            P("tp", None),
            P(None, "tp"),
            P("tp", None),
            P("grp", "tp"),
        ),
        out_specs=P("grp", "tp"),
        check_vma=False,
    )
```

```python
import functools
import math

import jax
import jax.numpy as jnp
from jax import lax
from jax.experimental import pallas as pl
from jax.experimental.pallas import tpu as pltpu
from jax.sharding import PartitionSpec as P

LEN = 1024
K = 8192
TB = 512
EPS = 1e-06
STEP_A, STEP_F, STEP_Y, STEP_B = 0, 1, 2, 3
VMEM = 20 * 1024 * 1024
STEPS = (3, 3, 3, 3)
DEPTH = 3

NT = (((1,), (1,)), ((), ()))
NN = (((1,), (0,)), ((), ()))


def mm(a, b, dims):
    return lax.dot_general(a, b, dims, preferred_element_type=jnp.float32)


def halves(a):
    hi = a.astype(jnp.bfloat16)
    lo = (a - hi.astype(jnp.float32)).astype(jnp.bfloat16)
    return jnp.concatenate([hi, lo], 0)


def rows_kernel(where_ref, x_ref, g_ref, a_ref, b_ref, keep_ref, send_ref, xs_ref, gs_ref, at_ref, bs_ref, sem, sem_w):
    first = where_ref[0] == 0
    per = keep_ref.shape[2] // TB
    weights = [
        pltpu.make_async_copy(src, dst, sem_w.at[j])
        for j, (src, dst) in enumerate(((a_ref, at_ref), (b_ref, bs_ref)))
    ]
    for copy in weights:
        copy.start()
    jobs, start = [], 0
    for c, blocks in enumerate(STEPS):
        rows = pl.ds(start * TB, blocks * TB)
        for j, (src, dst) in enumerate(((x_ref, xs_ref), (g_ref, gs_ref))):
            copy = pltpu.make_async_copy(src.at[rows], dst.at[rows], sem.at[j, c])
            jobs.append((j, range(start, start + blocks), copy))
        start += blocks
    for _, _, copy in jobs[:DEPTH]:
        copy.start()
    for copy in weights:
        copy.wait()
    for n, (j, blocks, copy) in enumerate(jobs):
        copy.wait()
        if n + DEPTH < len(jobs):
            jobs[n + DEPTH][2].start()
        for i in blocks:
            rows = slice(i * TB, (i + 1) * TB)
            cols = slice(i % per * TB, (i % per + 1) * TB)
            slot = (i // per - where_ref[2]) & 3
            if j == 0:
                keep_ref[slot, :, cols] = mm(at_ref[...], xs_ref[rows], NT)
            else:
                down = keep_ref[slot, :, cols]
                up = mm(bs_ref[...], gs_ref[rows], NT)
                keep_ref[slot, :, cols] = jnp.where(first, down, up)
                send_ref[slot, :, cols] = jnp.where(first, up, down)


def rank_rows(where, x, g, a, b):
    tokens, width = x.shape
    rank = b.shape[0]
    chunk = tokens // 4
    out = jax.ShapeDtypeStruct((4, rank, chunk), jnp.float32)
    near = pltpu.VMEM((tokens, width), jnp.bfloat16)
    whole = pl.BlockSpec(memory_space=pltpu.VMEM)
    far = pl.BlockSpec(memory_space=pl.ANY)
    x, g, a, b = (pltpu.with_memory_space_constraint(v, pltpu.HBM) for v in (x, g, a, b))
    return pl.pallas_call(
        rows_kernel,
        in_specs=[pl.BlockSpec(memory_space=pltpu.SMEM), far, far, far, far],
        out_specs=[whole] * 4,
        out_shape=[out, out, near, near],
        scratch_shapes=[
            pltpu.VMEM((rank, width), jnp.bfloat16),
            pltpu.VMEM((rank, width), jnp.bfloat16),
            pltpu.SemaphoreType.DMA((2, len(STEPS))),
            pltpu.SemaphoreType.DMA((2,)),
        ],
        compiler_params=pltpu.CompilerParams(vmem_limit_bytes=VMEM),
        cost_estimate=pl.CostEstimate(
            flops=4 * tokens * width * rank, bytes_accessed=4 * tokens * width, transcendentals=0
        ),
        name="rank_rows",
    )(where, x, g, a, b)


def share_kernel(where_ref, x_ref, g_ref, *refs):
    own_refs, (other_ref, s_ref, keep_ref, send_ref, v_ref) = refs[:4], refs[4:]
    rank, chunk = own_refs[0].shape
    per = chunk // TB
    first = where_ref[0] == 0
    for j, own_ref in enumerate(own_refs):
        begin = ((where_ref[2] - j) & 3) * per
        for c in range(per):
            rows = pl.ds(pl.multiple_of((begin + c) * TB, TB), TB)
            cols = slice(c * TB, (c + 1) * TB)
            own, other = own_ref[:, cols], other_ref[j, :, cols]
            a = mm(halves(jnp.where(first, other, own)), x_ref[rows], NN)
            b = mm(halves(jnp.where(first, own, other)), g_ref[rows], NN)
            v_ref[0, begin + c] = a[:rank] + a[rank:]
            v_ref[1, begin + c] = b[:rank] + b[rank:]
    sign = (2 * s_ref[...] - 1).astype(jnp.float32).astype(jnp.bfloat16)
    each = keep_ref.shape[0] // 2
    blocks, step = v_ref.shape[1], LEN // TB
    pad = jnp.zeros((128 - blocks // step * rank, x_ref.shape[1]), jnp.float32)
    for m in range(2):
        v = [sum(v_ref[m, i + k] for k in range(step)) for i in range(0, blocks, step)]
        f = mm(halves(jnp.concatenate(v + [pad], 0)), sign, NN)
        f = jnp.transpose(f[:128] + f[128:]).reshape(each, 2, -1, 128)
        for n in range(each):
            keep_ref[m * each + n] = jnp.where(first, f[n, 0], f[n, 1])
            send_ref[m * each + n] = jnp.where(first, f[n, 1], f[n, 0])


def feature_shares(where, x, g, own, other, bits, parts):
    tokens, width = x.shape
    rank = own[0].shape[0]
    kd = bits.shape[1]
    whole = pl.BlockSpec(memory_space=pltpu.VMEM)
    x, g = (pltpu.with_memory_space_constraint(v, pltpu.VMEM) for v in (x, g))
    return pl.pallas_call(
        share_kernel,
        in_specs=[pl.BlockSpec(memory_space=pltpu.SMEM)] + [whole] * (len(own) + 4),
        out_specs=[whole] * 2,
        out_shape=[jax.ShapeDtypeStruct((parts // 2, 2 * kd // parts, 128), jnp.float32)] * 2,
        scratch_shapes=[pltpu.VMEM((2, tokens // TB, rank, width), jnp.float32)],
        compiler_params=pltpu.CompilerParams(vmem_limit_bytes=VMEM),
        cost_estimate=pl.CostEstimate(
            flops=8 * tokens * width * rank, bytes_accessed=4 * tokens * width, transcendentals=0
        ),
        name="feature_shares",
    )(where, x, g, *own, other, bits)


def valid_kernel(rank, v_ref, hl_ref, sq_ref):
    v = v_ref[...]
    rows, cols = v.shape
    ks = cols // rank
    goes = lax.broadcasted_iota(jnp.int32, (cols, cols), 0)
    came = lax.broadcasted_iota(jnp.int32, (cols, cols), 1)
    move = jnp.where((came % rank) * ks + came // rank == goes, 1.0, 0.0).astype(jnp.bfloat16)
    hl_ref[...] = mm(move, halves(v), NT).astype(jnp.bfloat16)
    total = mm(jnp.ones((8, cols), jnp.bfloat16), halves(v * v), NT)
    sq_ref[...] = total[:, :rows] + total[:, rows:]


def valid_terms(v, rank):
    rows, cols = v.shape
    whole = pl.BlockSpec(memory_space=pltpu.VMEM)
    return pl.pallas_call(
        functools.partial(valid_kernel, rank),
        in_specs=[whole],
        out_specs=[whole, whole],
        out_shape=[
            jax.ShapeDtypeStruct((cols, 2 * rows), jnp.bfloat16),
            jax.ShapeDtypeStruct((8, rows), jnp.float32),
        ],
        compiler_params=pltpu.CompilerParams(vmem_limit_bytes=VMEM // 2),
        cost_estimate=pl.CostEstimate(
            flops=4 * rows * cols * cols, bytes_accessed=8 * rows * cols, transcendentals=0
        ),
        name="valid_terms",
    )(v)


def flip(step, z, y):
    if step == STEP_A:
        return z ^ 1, y
    if step == STEP_F:
        return z ^ 4, y
    if step == STEP_Y:
        return z, y ^ 1
    return (z + 2 * (z & 1) - 1) & 7, y


def flips(step):
    pairs = []
    for i in range(16):
        z, y = flip(step, i >> 1, i & 1)
        pairs.append((i, z * 2 + y))
    return pairs


def origin(place, index):
    z, y = index >> 1, index & 1
    for step in (3, 2, 1, 0):
        if place >> step & 1:
            z, y = flip(step, z, y)
    return z * 2 + y


def dot_kernel(rank, where_ref, f_ref, hl0_ref, sq0_ref, hl1_ref, sq1_ref, out_ref, t_ref):
    parts = out_ref.shape[0]
    rows = sq0_ref.shape[1]
    each = 2 * rows // parts
    t_ref[...] = jnp.transpose(jnp.sum(f_ref[...], 0))
    f = jnp.concatenate([t_ref[pl.ds(r, 8, stride=rank), :] for r in range(rank)], 1)
    own_sq = jnp.broadcast_to(jnp.sum(f * f, 1, keepdims=True), (8, each))
    f = halves(f)
    for half, (hl_ref, sq_ref) in enumerate(((hl0_ref, sq0_ref), (hl1_ref, sq1_ref))):
        prod = mm(f, hl_ref[...], NN)
        dots = prod[:8, :rows] + (prod[8:, :rows] + prod[:8, rows:]) + prod[8:, rows:]
        line = lax.broadcasted_iota(jnp.int32, dots.shape, 0)
        dots = jnp.where(line == 6, sq_ref[...], dots)
        for n in range(parts // 2):
            part = origin(half * parts // 2 + n, where_ref[1])
            out_ref[part, :, :each] = dots[:, n * each : (n + 1) * each]
            out_ref[part, :, each : 2 * each] = own_sq


def partial_dots(where, f, terms, rank):
    whole = pl.BlockSpec(memory_space=pltpu.VMEM)
    return pl.pallas_call(
        functools.partial(dot_kernel, rank),
        in_specs=[pl.BlockSpec(memory_space=pltpu.SMEM)] + [whole] * 5,
        out_specs=whole,
        out_shape=jax.ShapeDtypeStruct((2 * f.shape[0], 8, 128), jnp.float32),
        scratch_shapes=[pltpu.VMEM((128, f.shape[1]), jnp.float32)],
        compiler_params=pltpu.CompilerParams(vmem_limit_bytes=VMEM // 2),
        name="partial_dots",
    )(where, f, *terms)


def on_device(x, g, a, b, bits, valid):
    tp = lax.axis_size("tp")
    rank = b.shape[0]
    seqs = x.shape[0] // LEN
    each = 16 * valid.shape[0] // tp
    index = lax.axis_index("tp")
    where = jnp.stack([index & 1, lax.axis_index("grp"), index >> 1 & 3]).astype(jnp.int32)
    swap_core = [(i, i ^ 1) for i in range(tp)]
    swap_y = [(i, i ^ 8) for i in range(tp)]
    same_core = [list(range(c, tp, 2)) for c in range(2)]
    turn_x = [[(i, (i & 9) | (((i >> 1) + k & 3) << 1)) for i in range(tp)] for k in range(4)]

    def gather(step, rows):
        return rows, lax.ppermute(rows, "grp", flips(step))

    tie = lax.optimization_barrier

    def from_group(step, rows):
        return lax.ppermute(rows, "grp", flips(step))

    keep, send, x, g = rank_rows(where, x, g, jnp.transpose(a), b)
    send, near = tie((send, valid))
    far = from_group(STEP_A, near)
    mine = keep + lax.ppermute(send, "tp", swap_core)
    came = [lax.ppermute(mine[k], "tp", turn_x[k]) for k in (1, 2, 3)]
    came[0], near = tie((came[0], jnp.concatenate([near, far], 0)))
    far = from_group(STEP_F, near)
    mine = mine[0] + came[0] + came[1] + came[2]
    mine = mine + lax.ppermute(mine, "tp", swap_y)
    mine, near = tie((mine, jnp.concatenate([near, far], 0)))
    own = [mine] + [lax.ppermute(mine, "tp", turn_x[k]) for k in (1, 2, 3)]
    far = from_group(STEP_Y, near)
    own, near = tie((own, jnp.concatenate([near, far], 0)))
    far = from_group(STEP_B, near)
    other = lax.ppermute(jnp.stack(own), "tp", swap_core)
    near = valid_terms(near, rank)
    other, near = tie((other, near))
    keep, send = feature_shares(where, x, g, own, other, bits, tp)
    came = lax.ppermute(send, "tp", swap_core)
    shares = lax.all_to_all(keep + came, "tp", 0, 0, axis_index_groups=same_core, tiled=True)
    far = valid_terms(far, rank)
    dots = partial_dots(where, shares, [*near, *far], rank)
    dots = lax.all_to_all(dots, "tp", 0, 0, tiled=True)
    total = jnp.sum(dots, 0)
    train = math.sqrt(K) / jnp.sqrt(total[:seqs, each : 2 * each] + EPS)
    return total[:seqs, :each] * train / jnp.sqrt(total[6:7, :each] + EPS)


def solution(mesh):
    return jax.shard_map(
        on_device,
        mesh=mesh,
        in_specs=(
            P("grp", "tp"),
            P("grp", "tp"),
            P("tp", None),
            P(None, "tp"),
            P("tp", None),
            P("grp", "tp"),
        ),
        out_specs=P("grp", "tp"),
        check_vma=False,
    )
```

```python
import functools
import math

import jax
import jax.numpy as jnp
from jax import lax
from jax.experimental import pallas as pl
from jax.experimental.pallas import tpu as pltpu
from jax.sharding import PartitionSpec as P

LEN = 1024
K = 8192
TB = 512
EPS = 1e-06
STEP_A, STEP_F, STEP_B, STEP_Y = 0, 1, 2, 3
VMEM = 20 * 1024 * 1024
STEPS = (4, 4, 4)
DEPTH = 3

NT = (((1,), (1,)), ((), ()))
NN = (((1,), (0,)), ((), ()))


def mm(a, b, dims):
    return lax.dot_general(a, b, dims, preferred_element_type=jnp.float32)


def halves(a):
    hi = a.astype(jnp.bfloat16)
    lo = (a - hi.astype(jnp.float32)).astype(jnp.bfloat16)
    return jnp.concatenate([hi, lo], 0)


def rows_kernel(where_ref, x_ref, g_ref, a_ref, b_ref, keep_ref, send_ref, xs_ref, gs_ref, at_ref, bs_ref, sem, sem_w):
    first = where_ref[0] == 0
    per = keep_ref.shape[2] // TB
    weights = [
        pltpu.make_async_copy(src, dst, sem_w.at[j])
        for j, (src, dst) in enumerate(((a_ref, at_ref), (b_ref, bs_ref)))
    ]
    for copy in weights:
        copy.start()
    jobs, start = [], 0
    for c, blocks in enumerate(STEPS):
        rows = pl.ds(start * TB, blocks * TB)
        for j, (src, dst) in enumerate(((x_ref, xs_ref), (g_ref, gs_ref))):
            copy = pltpu.make_async_copy(src.at[rows], dst.at[rows], sem.at[j, c])
            jobs.append((j, range(start, start + blocks), copy))
        start += blocks
    for _, _, copy in jobs[:DEPTH]:
        copy.start()
    for copy in weights:
        copy.wait()
    for n, (j, blocks, copy) in enumerate(jobs):
        copy.wait()
        if n + DEPTH < len(jobs):
            jobs[n + DEPTH][2].start()
        for i in blocks:
            rows = slice(i * TB, (i + 1) * TB)
            cols = slice(i % per * TB, (i % per + 1) * TB)
            slot = (i // per - where_ref[2]) & 3
            if j == 0:
                keep_ref[slot, :, cols] = mm(at_ref[...], xs_ref[rows], NT)
            else:
                down = keep_ref[slot, :, cols]
                up = mm(bs_ref[...], gs_ref[rows], NT)
                keep_ref[slot, :, cols] = jnp.where(first, down, up)
                send_ref[slot, :, cols] = jnp.where(first, up, down)


def rank_rows(where, x, g, a, b):
    tokens, width = x.shape
    rank = b.shape[0]
    chunk = tokens // 4
    out = jax.ShapeDtypeStruct((4, rank, chunk), jnp.float32)
    near = pltpu.VMEM((tokens, width), jnp.bfloat16)
    whole = pl.BlockSpec(memory_space=pltpu.VMEM)
    far = pl.BlockSpec(memory_space=pl.ANY)
    x, g, a, b = (pltpu.with_memory_space_constraint(v, pltpu.HBM) for v in (x, g, a, b))
    return pl.pallas_call(
        rows_kernel,
        in_specs=[pl.BlockSpec(memory_space=pltpu.SMEM), far, far, far, far],
        out_specs=[whole] * 4,
        out_shape=[out, out, near, near],
        scratch_shapes=[
            pltpu.VMEM((rank, width), jnp.bfloat16),
            pltpu.VMEM((rank, width), jnp.bfloat16),
            pltpu.SemaphoreType.DMA((2, len(STEPS))),
            pltpu.SemaphoreType.DMA((2,)),
        ],
        compiler_params=pltpu.CompilerParams(vmem_limit_bytes=VMEM),
        cost_estimate=pl.CostEstimate(
            flops=4 * tokens * width * rank, bytes_accessed=4 * tokens * width, transcendentals=0
        ),
        name="rank_rows",
    )(where, x, g, a, b)


def share_kernel(where_ref, x_ref, g_ref, *refs):
    own_refs, (other_ref, s_ref, keep_ref, send_ref, v_ref) = refs[:4], refs[4:]
    rank, chunk = own_refs[0].shape
    per = chunk // TB
    first = where_ref[0] == 0
    for j, own_ref in enumerate(own_refs):
        begin = ((where_ref[2] - j) & 3) * per
        for c in range(per):
            rows = pl.ds(pl.multiple_of((begin + c) * TB, TB), TB)
            cols = slice(c * TB, (c + 1) * TB)
            own, other = own_ref[:, cols], other_ref[j, :, cols]
            a = mm(halves(jnp.where(first, other, own)), x_ref[rows], NN)
            b = mm(halves(jnp.where(first, own, other)), g_ref[rows], NN)
            v_ref[0, begin + c] = a[:rank] + a[rank:]
            v_ref[1, begin + c] = b[:rank] + b[rank:]
    sign = (2 * s_ref[...] - 1).astype(jnp.float32).astype(jnp.bfloat16)
    each = keep_ref.shape[0] // 2
    blocks, step = v_ref.shape[1], LEN // TB
    pad = jnp.zeros((128 - blocks // step * rank, x_ref.shape[1]), jnp.float32)
    for m in range(2):
        v = [sum(v_ref[m, i + k] for k in range(step)) for i in range(0, blocks, step)]
        f = mm(halves(jnp.concatenate(v + [pad], 0)), sign, NN)
        f = jnp.transpose(f[:128] + f[128:]).reshape(each, 2, -1, 128)
        for n in range(each):
            keep_ref[m * each + n] = jnp.where(first, f[n, 0], f[n, 1])
            send_ref[m * each + n] = jnp.where(first, f[n, 1], f[n, 0])


def feature_shares(where, x, g, own, other, bits, parts):
    tokens, width = x.shape
    rank = own[0].shape[0]
    kd = bits.shape[1]
    whole = pl.BlockSpec(memory_space=pltpu.VMEM)
    x, g = (pltpu.with_memory_space_constraint(v, pltpu.VMEM) for v in (x, g))
    return pl.pallas_call(
        share_kernel,
        in_specs=[pl.BlockSpec(memory_space=pltpu.SMEM)] + [whole] * (len(own) + 4),
        out_specs=[whole] * 2,
        out_shape=[jax.ShapeDtypeStruct((parts // 2, 2 * kd // parts, 128), jnp.float32)] * 2,
        scratch_shapes=[pltpu.VMEM((2, tokens // TB, rank, width), jnp.float32)],
        compiler_params=pltpu.CompilerParams(vmem_limit_bytes=VMEM),
        cost_estimate=pl.CostEstimate(
            flops=8 * tokens * width * rank, bytes_accessed=4 * tokens * width, transcendentals=0
        ),
        name="feature_shares",
    )(where, x, g, *own, other, bits)


def valid_kernel(rank, v_ref, hl_ref, sq_ref):
    v = v_ref[...]
    rows, cols = v.shape
    ks = cols // rank
    goes = lax.broadcasted_iota(jnp.int32, (cols, cols), 0)
    came = lax.broadcasted_iota(jnp.int32, (cols, cols), 1)
    move = jnp.where((came % rank) * ks + came // rank == goes, 1.0, 0.0).astype(jnp.bfloat16)
    hl_ref[...] = mm(move, halves(v), NT).astype(jnp.bfloat16)
    total = mm(jnp.ones((8, cols), jnp.bfloat16), halves(v * v), NT)
    sq_ref[...] = total[:, :rows] + total[:, rows:]


def valid_terms(v, rank):
    rows, cols = v.shape
    whole = pl.BlockSpec(memory_space=pltpu.VMEM)
    return pl.pallas_call(
        functools.partial(valid_kernel, rank),
        in_specs=[whole],
        out_specs=[whole, whole],
        out_shape=[
            jax.ShapeDtypeStruct((cols, 2 * rows), jnp.bfloat16),
            jax.ShapeDtypeStruct((8, rows), jnp.float32),
        ],
        compiler_params=pltpu.CompilerParams(vmem_limit_bytes=VMEM // 2),
        cost_estimate=pl.CostEstimate(
            flops=4 * rows * cols * cols, bytes_accessed=8 * rows * cols, transcendentals=0
        ),
        name="valid_terms",
    )(v)


def flip(step, z, y):
    if step == STEP_A:
        return z ^ 1, y
    if step == STEP_F:
        return z ^ 4, y
    if step == STEP_Y:
        return z, y ^ 1
    return (z + 2 * (z & 1) - 1) & 7, y


def flips(step):
    pairs = []
    for i in range(16):
        z, y = flip(step, i >> 1, i & 1)
        pairs.append((i, z * 2 + y))
    return pairs


def origin(place, index):
    z, y = index >> 1, index & 1
    for step in (3, 2, 1, 0):
        if place >> step & 1:
            z, y = flip(step, z, y)
    return z * 2 + y


def dot_kernel(rank, where_ref, f_ref, hl0_ref, sq0_ref, hl1_ref, sq1_ref, out_ref, t_ref):
    parts = out_ref.shape[0]
    rows = sq0_ref.shape[1]
    each = 2 * rows // parts
    t_ref[...] = jnp.transpose(jnp.sum(f_ref[...], 0))
    f = jnp.concatenate([t_ref[pl.ds(r, 8, stride=rank), :] for r in range(rank)], 1)
    own_sq = jnp.broadcast_to(jnp.sum(f * f, 1, keepdims=True), (8, each))
    f = halves(f)
    for half, (hl_ref, sq_ref) in enumerate(((hl0_ref, sq0_ref), (hl1_ref, sq1_ref))):
        prod = mm(f, hl_ref[...], NN)
        dots = prod[:8, :rows] + (prod[8:, :rows] + prod[:8, rows:]) + prod[8:, rows:]
        line = lax.broadcasted_iota(jnp.int32, dots.shape, 0)
        dots = jnp.where(line == 6, sq_ref[...], dots)
        for n in range(parts // 2):
            part = origin(half * parts // 2 + n, where_ref[1])
            out_ref[part, :, :each] = dots[:, n * each : (n + 1) * each]
            out_ref[part, :, each : 2 * each] = own_sq


def partial_dots(where, f, terms, rank):
    whole = pl.BlockSpec(memory_space=pltpu.VMEM)
    return pl.pallas_call(
        functools.partial(dot_kernel, rank),
        in_specs=[pl.BlockSpec(memory_space=pltpu.SMEM)] + [whole] * 5,
        out_specs=whole,
        out_shape=jax.ShapeDtypeStruct((2 * f.shape[0], 8, 128), jnp.float32),
        scratch_shapes=[pltpu.VMEM((128, f.shape[1]), jnp.float32)],
        compiler_params=pltpu.CompilerParams(vmem_limit_bytes=VMEM // 2),
        name="partial_dots",
    )(where, f, *terms)


def on_device(x, g, a, b, bits, valid):
    tp = lax.axis_size("tp")
    rank = b.shape[0]
    seqs = x.shape[0] // LEN
    each = 16 * valid.shape[0] // tp
    index = lax.axis_index("tp")
    where = jnp.stack([index & 1, lax.axis_index("grp"), index >> 1 & 3]).astype(jnp.int32)
    swap_core = [(i, i ^ 1) for i in range(tp)]
    swap_y = [(i, i ^ 8) for i in range(tp)]
    same_core = [list(range(c, tp, 2)) for c in range(2)]
    turn_x = [[(i, (i & 9) | (((i >> 1) + k & 3) << 1)) for i in range(tp)] for k in range(4)]

    def gather(step, rows):
        return rows, lax.ppermute(rows, "grp", flips(step))

    tie = lax.optimization_barrier

    def from_group(step, rows):
        return lax.ppermute(rows, "grp", flips(step))

    keep, send, x, g = rank_rows(where, x, g, jnp.transpose(a), b)
    send, near = tie((send, valid))
    far = from_group(STEP_A, near)
    mine = keep + lax.ppermute(send, "tp", swap_core)
    came = [lax.ppermute(mine[k], "tp", turn_x[k]) for k in (1, 2, 3)]
    near = jnp.concatenate([near, far], 0)
    far = from_group(STEP_F, near)
    mine = mine[0] + came[0] + came[1] + came[2]
    mine = mine + lax.ppermute(mine, "tp", swap_y)
    mine, near, far = tie((mine, near, far))
    near = jnp.concatenate([near, far], 0)
    own = [mine] + [lax.ppermute(mine, "tp", turn_x[k]) for k in (1, 2, 3)]
    far = from_group(STEP_B, near)
    own, near = tie((own, jnp.concatenate([near, far], 0)))
    far = from_group(STEP_Y, near)
    other = lax.ppermute(jnp.stack(own), "tp", swap_core)
    keep, send = feature_shares(where, x, g, own, other, bits, tp)
    send, near = tie((send, near))
    near = valid_terms(near, rank)
    came = lax.ppermute(send, "tp", swap_core)
    came, near = tie((came, near))
    shares = lax.all_to_all(keep + came, "tp", 0, 0, axis_index_groups=same_core, tiled=True)
    far = valid_terms(far, rank)
    dots = partial_dots(where, shares, [*near, *far], rank)
    dots = lax.all_to_all(dots, "tp", 0, 0, tiled=True)
    total = jnp.sum(dots, 0)
    train = math.sqrt(K) / jnp.sqrt(total[:seqs, each : 2 * each] + EPS)
    return total[:seqs, :each] * train / jnp.sqrt(total[6:7, :each] + EPS)


def solution(mesh):
    return jax.shard_map(
        on_device,
        mesh=mesh,
        in_specs=(
            P("grp", "tp"),
            P("grp", "tp"),
            P("tp", None),
            P(None, "tp"),
            P("tp", None),
            P("grp", "tp"),
        ),
        out_specs=P("grp", "tp"),
        check_vma=False,
    )
```

```python
import functools
import math

import jax
import jax.numpy as jnp
from jax import lax
from jax.experimental import pallas as pl
from jax.experimental.pallas import tpu as pltpu
from jax.sharding import PartitionSpec as P

LEN = 1024
K = 8192
TB = 512
EPS = 1e-06
STEP_A, STEP_F, STEP_B, STEP_Y = 0, 1, 2, 3
VMEM = 20 * 1024 * 1024
STEPS = (6, 6)
DEPTH = 2

NT = (((1,), (1,)), ((), ()))
NN = (((1,), (0,)), ((), ()))


def mm(a, b, dims):
    return lax.dot_general(a, b, dims, preferred_element_type=jnp.float32)


def halves(a):
    hi = a.astype(jnp.bfloat16)
    lo = (a - hi.astype(jnp.float32)).astype(jnp.bfloat16)
    return jnp.concatenate([hi, lo], 0)


def rows_kernel(x_ref, g_ref, a_ref, b_ref, keep_ref, send_ref, xs_ref, gs_ref, at_ref, bs_ref, sem, sem_w):
    first = (lax.axis_index("tp") & 1) == 0
    per = keep_ref.shape[2] // TB
    weights = [
        pltpu.make_async_copy(src, dst, sem_w.at[j])
        for j, (src, dst) in enumerate(((a_ref, at_ref), (b_ref, bs_ref)))
    ]
    for copy in weights:
        copy.start()
    jobs, start = [], 0
    for c, blocks in enumerate(STEPS):
        rows = pl.ds(start * TB, blocks * TB)
        for j, (src, dst) in enumerate(((x_ref, xs_ref), (g_ref, gs_ref))):
            copy = pltpu.make_async_copy(src.at[rows], dst.at[rows], sem.at[j, c])
            jobs.append((j, range(start, start + blocks), copy))
        start += blocks
    for _, _, copy in jobs[:DEPTH]:
        copy.start()
    for copy in weights:
        copy.wait()
    for n, (j, blocks, copy) in enumerate(jobs):
        copy.wait()
        if n + DEPTH < len(jobs):
            jobs[n + DEPTH][2].start()
        for i in blocks:
            rows = slice(i * TB, (i + 1) * TB)
            cols = slice(i % per * TB, (i % per + 1) * TB)
            slot = (i // per - (lax.axis_index("tp") >> 1 & 3)) & 3
            if j == 0:
                keep_ref[slot, :, cols] = mm(at_ref[...], xs_ref[rows], NT)
            else:
                down = keep_ref[slot, :, cols]
                up = mm(bs_ref[...], gs_ref[rows], NT)
                keep_ref[slot, :, cols] = jnp.where(first, down, up)
                send_ref[slot, :, cols] = jnp.where(first, up, down)


def rank_rows(x, g, a, b):
    tokens, width = x.shape
    rank = b.shape[0]
    chunk = tokens // 4
    out = jax.ShapeDtypeStruct((4, rank, chunk), jnp.float32)
    near = pltpu.VMEM((tokens, width), jnp.bfloat16)
    whole = pl.BlockSpec(memory_space=pltpu.VMEM)
    far = pl.BlockSpec(memory_space=pl.ANY)
    x, g, a, b = (pltpu.with_memory_space_constraint(v, pltpu.HBM) for v in (x, g, a, b))
    return pl.pallas_call(
        rows_kernel,
        in_specs=[far] * 4,
        out_specs=[whole] * 4,
        out_shape=[out, out, near, near],
        scratch_shapes=[
            pltpu.VMEM((rank, width), jnp.bfloat16),
            pltpu.VMEM((rank, width), jnp.bfloat16),
            pltpu.SemaphoreType.DMA((2, len(STEPS))),
            pltpu.SemaphoreType.DMA((2,)),
        ],
        compiler_params=pltpu.CompilerParams(vmem_limit_bytes=VMEM),
        cost_estimate=pl.CostEstimate(
            flops=4 * tokens * width * rank, bytes_accessed=4 * tokens * width, transcendentals=0
        ),
        name="rank_rows",
    )(x, g, a, b)


def share_kernel(x_ref, g_ref, *refs):
    own_refs, (other_ref, s_ref, keep_ref, send_ref, v_ref) = refs[:4], refs[4:]
    rank, chunk = own_refs[0].shape
    per = chunk // TB
    first = (lax.axis_index("tp") & 1) == 0
    for j, own_ref in enumerate(own_refs):
        begin = (((lax.axis_index("tp") >> 1 & 3) - j) & 3) * per
        for c in range(per):
            rows = pl.ds(pl.multiple_of((begin + c) * TB, TB), TB)
            cols = slice(c * TB, (c + 1) * TB)
            own, other = own_ref[:, cols], other_ref[j, :, cols]
            a = mm(halves(jnp.where(first, other, own)), x_ref[rows], NN)
            b = mm(halves(jnp.where(first, own, other)), g_ref[rows], NN)
            v_ref[0, begin + c] = a[:rank] + a[rank:]
            v_ref[1, begin + c] = b[:rank] + b[rank:]
    sign = (2 * s_ref[...] - 1).astype(jnp.float32).astype(jnp.bfloat16)
    each = keep_ref.shape[0] // 2
    blocks, step = v_ref.shape[1], LEN // TB
    pad = jnp.zeros((128 - blocks // step * rank, x_ref.shape[1]), jnp.float32)
    for m in range(2):
        v = [sum(v_ref[m, i + k] for k in range(step)) for i in range(0, blocks, step)]
        f = mm(halves(jnp.concatenate(v + [pad], 0)), sign, NN)
        f = jnp.transpose(f[:128] + f[128:]).reshape(each, 2, -1, 128)
        for n in range(each):
            keep_ref[m * each + n] = jnp.where(first, f[n, 0], f[n, 1])
            send_ref[m * each + n] = jnp.where(first, f[n, 1], f[n, 0])


def feature_shares(x, g, own, other, bits, parts):
    tokens, width = x.shape
    rank = own[0].shape[0]
    kd = bits.shape[1]
    whole = pl.BlockSpec(memory_space=pltpu.VMEM)
    x, g = (pltpu.with_memory_space_constraint(v, pltpu.VMEM) for v in (x, g))
    return pl.pallas_call(
        share_kernel,
        in_specs=[whole] * (len(own) + 4),
        out_specs=[whole] * 2,
        out_shape=[jax.ShapeDtypeStruct((parts // 2, 2 * kd // parts, 128), jnp.float32)] * 2,
        scratch_shapes=[pltpu.VMEM((2, tokens // TB, rank, width), jnp.float32)],
        compiler_params=pltpu.CompilerParams(vmem_limit_bytes=VMEM),
        cost_estimate=pl.CostEstimate(
            flops=8 * tokens * width * rank, bytes_accessed=4 * tokens * width, transcendentals=0
        ),
        name="feature_shares",
    )(x, g, *own, other, bits)


def valid_kernel(rank, v_ref, hl_ref, sq_ref):
    v = v_ref[...]
    rows, cols = v.shape
    ks = cols // rank
    goes = lax.broadcasted_iota(jnp.int32, (cols, cols), 0)
    came = lax.broadcasted_iota(jnp.int32, (cols, cols), 1)
    move = jnp.where((came % rank) * ks + came // rank == goes, 1.0, 0.0).astype(jnp.bfloat16)
    hl_ref[...] = mm(move, halves(v), NT).astype(jnp.bfloat16)
    total = mm(jnp.ones((8, cols), jnp.bfloat16), halves(v * v), NT)
    sq_ref[...] = total[:, :rows] + total[:, rows:]


def valid_terms(v, rank):
    rows, cols = v.shape
    whole = pl.BlockSpec(memory_space=pltpu.VMEM)
    return pl.pallas_call(
        functools.partial(valid_kernel, rank),
        in_specs=[whole],
        out_specs=[whole, whole],
        out_shape=[
            jax.ShapeDtypeStruct((cols, 2 * rows), jnp.bfloat16),
            jax.ShapeDtypeStruct((8, rows), jnp.float32),
        ],
        compiler_params=pltpu.CompilerParams(vmem_limit_bytes=VMEM // 2),
        cost_estimate=pl.CostEstimate(
            flops=4 * rows * cols * cols, bytes_accessed=8 * rows * cols, transcendentals=0
        ),
        name="valid_terms",
    )(v)


def flip(step, z, y):
    if step == STEP_A:
        return z ^ 1, y
    if step == STEP_F:
        return z ^ 4, y
    if step == STEP_Y:
        return z, y ^ 1
    return (z + 2 * (z & 1) - 1) & 7, y


def flips(step):
    pairs = []
    for i in range(16):
        z, y = flip(step, i >> 1, i & 1)
        pairs.append((i, z * 2 + y))
    return pairs


def origin(place, index):
    z, y = index >> 1, index & 1
    for step in (3, 2, 1, 0):
        if place >> step & 1:
            z, y = flip(step, z, y)
    return z * 2 + y


def dot_kernel(rank, f_ref, hl0_ref, sq0_ref, hl1_ref, sq1_ref, out_ref, t_ref):
    parts = out_ref.shape[0]
    rows = sq0_ref.shape[1]
    each = 2 * rows // parts
    t_ref[...] = jnp.transpose(jnp.sum(f_ref[...], 0))
    f = jnp.concatenate([t_ref[pl.ds(r, 8, stride=rank), :] for r in range(rank)], 1)
    own_sq = jnp.broadcast_to(jnp.sum(f * f, 1, keepdims=True), (8, 128))
    lane = lax.broadcasted_iota(jnp.int32, (8, 128), 1)
    origins = [origin(n, lax.axis_index("grp")) for n in range(parts // 2)]
    f = halves(f)
    for half, (hl_ref, sq_ref) in enumerate(((hl0_ref, sq0_ref), (hl1_ref, sq1_ref))):
        prod = mm(f, hl_ref[...], NN)
        dots = prod[:8, :rows] + (prod[8:, :rows] + prod[:8, rows:]) + prod[8:, rows:]
        line = lax.broadcasted_iota(jnp.int32, dots.shape, 0)
        dots = jnp.where(line == 6, sq_ref[...], dots)
        for n, part in enumerate(origins):
            begin, turn = divmod(n * each, 128)
            tile = dots[:, begin * 128 : (begin + 1) * 128]
            if turn:
                tile = pltpu.roll(tile, 128 - turn, 1)
            out_ref[part ^ half] = jnp.where(lane < each, tile, own_sq)


def partial_dots(f, terms, rank):
    whole = pl.BlockSpec(memory_space=pltpu.VMEM)
    return pl.pallas_call(
        functools.partial(dot_kernel, rank),
        in_specs=[whole] * 5,
        out_specs=whole,
        out_shape=jax.ShapeDtypeStruct((2 * f.shape[0], 8, 128), jnp.float32),
        scratch_shapes=[pltpu.VMEM((128, f.shape[1]), jnp.float32)],
        compiler_params=pltpu.CompilerParams(vmem_limit_bytes=VMEM // 2),
        name="partial_dots",
    )(f, *terms)


def on_device(x, g, a, b, bits, valid):
    tp = lax.axis_size("tp")
    rank = b.shape[0]
    seqs = x.shape[0] // LEN
    each = 16 * valid.shape[0] // tp
    swap_core = [(i, i ^ 1) for i in range(tp)]
    swap_y = [(i, i ^ 8) for i in range(tp)]
    same_core = [list(range(c, tp, 2)) for c in range(2)]
    turn_x = [[(i, (i & 9) | (((i >> 1) + k & 3) << 1)) for i in range(tp)] for k in range(4)]

    def gather(step, rows):
        return rows, lax.ppermute(rows, "grp", flips(step))

    tie = lax.optimization_barrier

    def from_group(step, rows):
        return lax.ppermute(rows, "grp", flips(step))

    keep, send, x, g = rank_rows(x, g, jnp.transpose(a), b)
    send, near = tie((send, valid))
    far = from_group(STEP_A, near)
    mine = keep + lax.ppermute(send, "tp", swap_core)
    came = [lax.ppermute(mine[k], "tp", turn_x[k]) for k in (1, 2, 3)]
    near = jnp.concatenate([near, far], 0)
    far = from_group(STEP_F, near)
    mine = mine[0] + came[0] + came[1] + came[2]
    mine = mine + lax.ppermute(mine, "tp", swap_y)
    mine, near, far = tie((mine, near, far))
    near = jnp.concatenate([near, far], 0)
    own = [mine] + [lax.ppermute(mine, "tp", turn_x[k]) for k in (1, 2, 3)]
    far = from_group(STEP_B, near)
    own, near = tie((own, jnp.concatenate([near, far], 0)))
    far = from_group(STEP_Y, near)
    other = lax.ppermute(jnp.stack(own), "tp", swap_core)
    keep, send = feature_shares(x, g, own, other, bits, tp)
    send, near = tie((send, near))
    near = valid_terms(near, rank)
    came = lax.ppermute(send, "tp", swap_core)
    came, near = tie((came, near))
    shares = lax.all_to_all(keep + came, "tp", 0, 0, axis_index_groups=same_core, tiled=True)
    far = valid_terms(far, rank)
    dots = partial_dots(shares, [*near, *far], rank)
    dots = lax.all_to_all(dots, "tp", 0, 0, tiled=True)
    total = jnp.sum(dots, 0)
    train = math.sqrt(K) / jnp.sqrt(total[:seqs, each : 2 * each] + EPS)
    return total[:seqs, :each] * train / jnp.sqrt(total[6:7, :each] + EPS)


def solution(mesh):
    return jax.shard_map(
        on_device,
        mesh=mesh,
        in_specs=(
            P("grp", "tp"),
            P("grp", "tp"),
            P("tp", None),
            P(None, "tp"),
            P("tp", None),
            P("grp", "tp"),
        ),
        out_specs=P("grp", "tp"),
        check_vma=False,
    )
```

```python
import functools
import math

import jax
import jax.numpy as jnp
from jax import lax
from jax.experimental import pallas as pl
from jax.experimental.pallas import tpu as pltpu
from jax.sharding import PartitionSpec as P

LEN = 1024
K = 8192
TB = 512
EPS = 1e-06
STEP_B, STEP_F, STEP_A, STEP_Y = 0, 1, 2, 3
VMEM = 20 * 1024 * 1024
STEPS = (6, 6)
DEPTH = 2

NT = (((1,), (1,)), ((), ()))
NN = (((1,), (0,)), ((), ()))


def mm(a, b, dims):
    return lax.dot_general(a, b, dims, preferred_element_type=jnp.float32)


def halves(a):
    hi = a.astype(jnp.bfloat16)
    lo = (a - hi.astype(jnp.float32)).astype(jnp.bfloat16)
    return jnp.concatenate([hi, lo], 0)


def rows_kernel(x_ref, g_ref, a_ref, b_ref, keep_ref, send_ref, xs_ref, gs_ref, at_ref, bs_ref, sem, sem_w):
    first = (lax.axis_index("tp") & 1) == 0
    per = keep_ref.shape[2] // TB
    weights = [
        pltpu.make_async_copy(src, dst, sem_w.at[j])
        for j, (src, dst) in enumerate(((a_ref, at_ref), (b_ref, bs_ref)))
    ]
    for copy in weights:
        copy.start()
    jobs, start = [], 0
    for c, blocks in enumerate(STEPS):
        rows = pl.ds(start * TB, blocks * TB)
        for j, (src, dst) in enumerate(((x_ref, xs_ref), (g_ref, gs_ref))):
            copy = pltpu.make_async_copy(src.at[rows], dst.at[rows], sem.at[j, c])
            jobs.append((j, range(start, start + blocks), copy))
        start += blocks
    for _, _, copy in jobs[:DEPTH]:
        copy.start()
    for copy in weights:
        copy.wait()
    for n, (j, blocks, copy) in enumerate(jobs):
        copy.wait()
        if n + DEPTH < len(jobs):
            jobs[n + DEPTH][2].start()
        for i in blocks:
            rows = slice(i * TB, (i + 1) * TB)
            cols = slice(i % per * TB, (i % per + 1) * TB)
            slot = (i // per - (lax.axis_index("tp") >> 1 & 3)) & 3
            if j == 0:
                keep_ref[slot, :, cols] = mm(at_ref[...], xs_ref[rows], NT)
            else:
                down = keep_ref[slot, :, cols]
                up = mm(bs_ref[...], gs_ref[rows], NT)
                keep_ref[slot, :, cols] = jnp.where(first, down, up)
                send_ref[slot, :, cols] = jnp.where(first, up, down)


def rank_rows(x, g, a, b):
    tokens, width = x.shape
    rank = b.shape[0]
    chunk = tokens // 4
    out = jax.ShapeDtypeStruct((4, rank, chunk), jnp.float32)
    near = pltpu.VMEM((tokens, width), jnp.bfloat16)
    whole = pl.BlockSpec(memory_space=pltpu.VMEM)
    far = pl.BlockSpec(memory_space=pl.ANY)
    x, g, a, b = (pltpu.with_memory_space_constraint(v, pltpu.HBM) for v in (x, g, a, b))
    return pl.pallas_call(
        rows_kernel,
        in_specs=[far] * 4,
        out_specs=[whole] * 4,
        out_shape=[out, out, near, near],
        scratch_shapes=[
            pltpu.VMEM((rank, width), jnp.bfloat16),
            pltpu.VMEM((rank, width), jnp.bfloat16),
            pltpu.SemaphoreType.DMA((2, len(STEPS))),
            pltpu.SemaphoreType.DMA((2,)),
        ],
        compiler_params=pltpu.CompilerParams(vmem_limit_bytes=VMEM),
        cost_estimate=pl.CostEstimate(
            flops=4 * tokens * width * rank, bytes_accessed=4 * tokens * width, transcendentals=0
        ),
        name="rank_rows",
    )(x, g, a, b)


def share_kernel(x_ref, g_ref, *refs):
    own_refs, (other_ref, s_ref, keep_ref, send_ref, v_ref) = refs[:4], refs[4:]
    rank, chunk = own_refs[0].shape
    per = chunk // TB
    first = (lax.axis_index("tp") & 1) == 0
    for j, own_ref in enumerate(own_refs):
        begin = (((lax.axis_index("tp") >> 1 & 3) - j) & 3) * per
        for c in range(per):
            rows = pl.ds(pl.multiple_of((begin + c) * TB, TB), TB)
            cols = slice(c * TB, (c + 1) * TB)
            own, other = own_ref[:, cols], other_ref[j, :, cols]
            a = mm(halves(jnp.where(first, other, own)), x_ref[rows], NN)
            b = mm(halves(jnp.where(first, own, other)), g_ref[rows], NN)
            v_ref[0, begin + c] = a[:rank] + a[rank:]
            v_ref[1, begin + c] = b[:rank] + b[rank:]
    sign = (2 * s_ref[...] - 1).astype(jnp.float32).astype(jnp.bfloat16)
    each = keep_ref.shape[0] // 2
    blocks, step = v_ref.shape[1], LEN // TB
    pad = jnp.zeros((128 - blocks // step * rank, x_ref.shape[1]), jnp.float32)
    for m in range(2):
        v = [sum(v_ref[m, i + k] for k in range(step)) for i in range(0, blocks, step)]
        f = mm(halves(jnp.concatenate(v + [pad], 0)), sign, NN)
        f = jnp.transpose(f[:128] + f[128:]).reshape(each, 2, -1, 128)
        for n in range(each):
            keep_ref[m * each + n] = jnp.where(first, f[n, 0], f[n, 1])
            send_ref[m * each + n] = jnp.where(first, f[n, 1], f[n, 0])


def feature_shares(x, g, own, other, bits, parts):
    tokens, width = x.shape
    rank = own[0].shape[0]
    kd = bits.shape[1]
    whole = pl.BlockSpec(memory_space=pltpu.VMEM)
    x, g = (pltpu.with_memory_space_constraint(v, pltpu.VMEM) for v in (x, g))
    return pl.pallas_call(
        share_kernel,
        in_specs=[whole] * (len(own) + 4),
        out_specs=[whole] * 2,
        out_shape=[jax.ShapeDtypeStruct((parts // 2, 2 * kd // parts, 128), jnp.float32)] * 2,
        scratch_shapes=[pltpu.VMEM((2, tokens // TB, rank, width), jnp.float32)],
        compiler_params=pltpu.CompilerParams(vmem_limit_bytes=VMEM),
        cost_estimate=pl.CostEstimate(
            flops=8 * tokens * width * rank, bytes_accessed=4 * tokens * width, transcendentals=0
        ),
        name="feature_shares",
    )(x, g, *own, other, bits)


def valid_kernel(rank, v_ref, hl_ref, sq_ref):
    v = v_ref[...]
    rows, cols = v.shape
    ks = cols // rank
    goes = lax.broadcasted_iota(jnp.int32, (cols, cols), 0)
    came = lax.broadcasted_iota(jnp.int32, (cols, cols), 1)
    move = jnp.where((came % rank) * ks + came // rank == goes, 1.0, 0.0).astype(jnp.bfloat16)
    hl_ref[...] = mm(move, halves(v), NT).astype(jnp.bfloat16)
    total = mm(jnp.ones((8, cols), jnp.bfloat16), halves(v * v), NT)
    sq_ref[...] = total[:, :rows] + total[:, rows:]


def valid_terms(v, rank):
    rows, cols = v.shape
    whole = pl.BlockSpec(memory_space=pltpu.VMEM)
    return pl.pallas_call(
        functools.partial(valid_kernel, rank),
        in_specs=[whole],
        out_specs=[whole, whole],
        out_shape=[
            jax.ShapeDtypeStruct((cols, 2 * rows), jnp.bfloat16),
            jax.ShapeDtypeStruct((8, rows), jnp.float32),
        ],
        compiler_params=pltpu.CompilerParams(vmem_limit_bytes=VMEM // 2),
        cost_estimate=pl.CostEstimate(
            flops=4 * rows * cols * cols, bytes_accessed=8 * rows * cols, transcendentals=0
        ),
        name="valid_terms",
    )(v)


def flip(step, z, y):
    if step == STEP_A:
        return z ^ 1, y
    if step == STEP_F:
        return z ^ 4, y
    if step == STEP_Y:
        return z, y ^ 1
    return (z + 2 * (z & 1) - 1) & 7, y


def flips(step):
    pairs = []
    for i in range(16):
        z, y = flip(step, i >> 1, i & 1)
        pairs.append((i, z * 2 + y))
    return pairs


def origin(place, index):
    z, y = index >> 1, index & 1
    for step in (3, 2, 1, 0):
        if place >> step & 1:
            z, y = flip(step, z, y)
    return z * 2 + y


def dot_kernel(rank, f_ref, hl0_ref, sq0_ref, hl1_ref, sq1_ref, out_ref, t_ref):
    parts = out_ref.shape[0]
    rows = sq0_ref.shape[1]
    each = 2 * rows // parts
    t_ref[...] = jnp.transpose(jnp.sum(f_ref[...], 0))
    f = jnp.concatenate([t_ref[pl.ds(r, 8, stride=rank), :] for r in range(rank)], 1)
    own_sq = jnp.broadcast_to(jnp.sum(f * f, 1, keepdims=True), (8, 128))
    lane = lax.broadcasted_iota(jnp.int32, (8, 128), 1)
    origins = [origin(n, lax.axis_index("grp")) for n in range(parts // 2)]
    f = halves(f)
    for half, (hl_ref, sq_ref) in enumerate(((hl0_ref, sq0_ref), (hl1_ref, sq1_ref))):
        prod = mm(f, hl_ref[...], NN)
        dots = prod[:8, :rows] + (prod[8:, :rows] + prod[:8, rows:]) + prod[8:, rows:]
        line = lax.broadcasted_iota(jnp.int32, dots.shape, 0)
        dots = jnp.where(line == 6, sq_ref[...], dots)
        for n, part in enumerate(origins):
            begin, turn = divmod(n * each, 128)
            tile = dots[:, begin * 128 : (begin + 1) * 128]
            if turn:
                tile = pltpu.roll(tile, 128 - turn, 1)
            out_ref[part ^ half] = jnp.where(lane < each, tile, own_sq)


def partial_dots(f, terms, rank):
    whole = pl.BlockSpec(memory_space=pltpu.VMEM)
    return pl.pallas_call(
        functools.partial(dot_kernel, rank),
        in_specs=[whole] * 5,
        out_specs=whole,
        out_shape=jax.ShapeDtypeStruct((2 * f.shape[0], 8, 128), jnp.float32),
        scratch_shapes=[pltpu.VMEM((128, f.shape[1]), jnp.float32)],
        compiler_params=pltpu.CompilerParams(vmem_limit_bytes=VMEM // 2),
        name="partial_dots",
    )(f, *terms)


def on_device(x, g, a, b, bits, valid):
    tp = lax.axis_size("tp")
    rank = b.shape[0]
    seqs = x.shape[0] // LEN
    each = 16 * valid.shape[0] // tp
    swap_core = [(i, i ^ 1) for i in range(tp)]
    swap_y = [(i, i ^ 8) for i in range(tp)]
    same_core = [list(range(c, tp, 2)) for c in range(2)]
    turn_x = [[(i, (i & 9) | (((i >> 1) + k & 3) << 1)) for i in range(tp)] for k in range(4)]

    def gather(step, rows):
        return rows, lax.ppermute(rows, "grp", flips(step))

    tie = lax.optimization_barrier

    def from_group(step, rows):
        return lax.ppermute(rows, "grp", flips(step))

    keep, send, x, g = rank_rows(x, g, jnp.transpose(a), b)
    send, near = tie((send, valid))
    far = from_group(STEP_B, near)
    mine = keep + lax.ppermute(send, "tp", swap_core)
    came = [lax.ppermute(mine[k], "tp", turn_x[k]) for k in (1, 2, 3)]
    near = jnp.concatenate([near, far], 0)
    far = from_group(STEP_F, near)
    mine = mine[0] + came[0] + came[1] + came[2]
    mine = mine + lax.ppermute(mine, "tp", swap_y)
    mine, near, far = tie((mine, near, far))
    near = jnp.concatenate([near, far], 0)
    own = [mine] + [lax.ppermute(mine, "tp", turn_x[k]) for k in (1, 2, 3)]
    far = from_group(STEP_A, near)
    own, near = tie((own, jnp.concatenate([near, far], 0)))
    far = from_group(STEP_Y, near)
    other = lax.ppermute(jnp.stack(own), "tp", swap_core)
    keep, send = feature_shares(x, g, own, other, bits, tp)
    send, near = tie((send, near))
    near = valid_terms(near, rank)
    came = lax.ppermute(send, "tp", swap_core)
    came, near = tie((came, near))
    shares = lax.all_to_all(keep + came, "tp", 0, 0, axis_index_groups=same_core, tiled=True)
    far = valid_terms(far, rank)
    dots = partial_dots(shares, [*near, *far], rank)
    dots = lax.all_to_all(dots, "tp", 0, 0, tiled=True)
    total = jnp.sum(dots, 0)
    train = math.sqrt(K) / jnp.sqrt(total[:seqs, each : 2 * each] + EPS)
    return total[:seqs, :each] * train / jnp.sqrt(total[6:7, :each] + EPS)


def solution(mesh):
    return jax.shard_map(
        on_device,
        mesh=mesh,
        in_specs=(
            P("grp", "tp"),
            P("grp", "tp"),
            P("tp", None),
            P(None, "tp"),
            P("tp", None),
            P("grp", "tp"),
        ),
        out_specs=P("grp", "tp"),
        check_vma=False,
    )
```

```python
import functools
import math

import jax
import jax.numpy as jnp
from jax import lax
from jax.experimental import pallas as pl
from jax.experimental.pallas import tpu as pltpu
from jax.sharding import PartitionSpec as P

LEN = 1024
K = 8192
TB = 512
EPS = 1e-06
STEP_B, STEP_F, STEP_A, STEP_Y = 0, 1, 2, 3
VMEM = 20 * 1024 * 1024
STEPS = (6, 6)
DEPTH = 2

NT = (((1,), (1,)), ((), ()))
NN = (((1,), (0,)), ((), ()))


def mm(a, b, dims):
    return lax.dot_general(a, b, dims, preferred_element_type=jnp.float32)


def halves(a):
    hi = a.astype(jnp.bfloat16)
    lo = (a - hi.astype(jnp.float32)).astype(jnp.bfloat16)
    return jnp.concatenate([hi, lo], 0)


def rows_kernel(x_ref, g_ref, a_ref, b_ref, keep_ref, send_ref, xs_ref, gs_ref, at_ref, bs_ref, sem, sem_w):
    first = (lax.axis_index("tp") & 1) == 0
    per = keep_ref.shape[2] // TB
    weights = [
        pltpu.make_async_copy(src, dst, sem_w.at[j])
        for j, (src, dst) in enumerate(((a_ref, at_ref), (b_ref, bs_ref)))
    ]
    for copy in weights:
        copy.start()
    jobs, start = [], 0
    for c, blocks in enumerate(STEPS):
        rows = pl.ds(start * TB, blocks * TB)
        for j, (src, dst) in enumerate(((x_ref, xs_ref), (g_ref, gs_ref))):
            copy = pltpu.make_async_copy(src.at[rows], dst.at[rows], sem.at[j, c])
            jobs.append((j, range(start, start + blocks), copy))
        start += blocks
    for _, _, copy in jobs[:DEPTH]:
        copy.start()
    for copy in weights:
        copy.wait()
    for n, (j, blocks, copy) in enumerate(jobs):
        copy.wait()
        if n + DEPTH < len(jobs):
            jobs[n + DEPTH][2].start()
        for i in blocks:
            rows = slice(i * TB, (i + 1) * TB)
            cols = slice(i % per * TB, (i % per + 1) * TB)
            slot = (i // per - (lax.axis_index("tp") >> 1 & 3)) & 3
            if j == 0:
                keep_ref[slot, :, cols] = mm(at_ref[...], xs_ref[rows], NT)
            else:
                down = keep_ref[slot, :, cols]
                up = mm(bs_ref[...], gs_ref[rows], NT)
                keep_ref[slot, :, cols] = jnp.where(first, down, up)
                send_ref[slot, :, cols] = jnp.where(first, up, down)


def rank_rows(x, g, a, b):
    tokens, width = x.shape
    rank = b.shape[0]
    chunk = tokens // 4
    out = jax.ShapeDtypeStruct((4, rank, chunk), jnp.float32)
    near = pltpu.VMEM((tokens, width), jnp.bfloat16)
    whole = pl.BlockSpec(memory_space=pltpu.VMEM)
    far = pl.BlockSpec(memory_space=pl.ANY)
    x, g, a, b = (pltpu.with_memory_space_constraint(v, pltpu.HBM) for v in (x, g, a, b))
    return pl.pallas_call(
        rows_kernel,
        in_specs=[far] * 4,
        out_specs=[whole] * 4,
        out_shape=[out, out, near, near],
        scratch_shapes=[
            pltpu.VMEM((rank, width), jnp.bfloat16),
            pltpu.VMEM((rank, width), jnp.bfloat16),
            pltpu.SemaphoreType.DMA((2, len(STEPS))),
            pltpu.SemaphoreType.DMA((2,)),
        ],
        compiler_params=pltpu.CompilerParams(vmem_limit_bytes=VMEM),
        cost_estimate=pl.CostEstimate(
            flops=4 * tokens * width * rank, bytes_accessed=4 * tokens * width, transcendentals=0
        ),
        name="rank_rows",
    )(x, g, a, b)


def share_kernel(x_ref, g_ref, *refs):
    own_refs, (other_ref, s_ref, keep_ref, send_ref, v_ref) = refs[:4], refs[4:]
    rank, chunk = own_refs[0].shape
    per = chunk // TB
    first = (lax.axis_index("tp") & 1) == 0
    for j, own_ref in enumerate(own_refs):
        begin = (((lax.axis_index("tp") >> 1 & 3) - j) & 3) * per
        for c in range(per):
            rows = pl.ds(pl.multiple_of((begin + c) * TB, TB), TB)
            cols = slice(c * TB, (c + 1) * TB)
            own, other = own_ref[:, cols], other_ref[j, :, cols]
            a = mm(halves(jnp.where(first, other, own)), x_ref[rows], NN)
            b = mm(halves(jnp.where(first, own, other)), g_ref[rows], NN)
            v_ref[0, begin + c] = a[:rank] + a[rank:]
            v_ref[1, begin + c] = b[:rank] + b[rank:]
    sign = s_ref[...]
    each = keep_ref.shape[0] // 2
    blocks, step = v_ref.shape[1], LEN // TB
    pad = jnp.zeros((128 - blocks // step * rank, x_ref.shape[1]), jnp.float32)
    for m in range(2):
        v = [sum(v_ref[m, i + k] for k in range(step)) for i in range(0, blocks, step)]
        f = mm(halves(jnp.concatenate(v + [pad], 0)), sign, NN)
        f = jnp.transpose(f[:128] + f[128:]).reshape(each, 2, -1, 128)
        for n in range(each):
            keep_ref[m * each + n] = jnp.where(first, f[n, 0], f[n, 1])
            send_ref[m * each + n] = jnp.where(first, f[n, 1], f[n, 0])


def feature_shares(x, g, own, other, bits, parts):
    tokens, width = x.shape
    rank = own[0].shape[0]
    kd = bits.shape[1]
    whole = pl.BlockSpec(memory_space=pltpu.VMEM)
    x, g = (pltpu.with_memory_space_constraint(v, pltpu.VMEM) for v in (x, g))
    return pl.pallas_call(
        share_kernel,
        in_specs=[whole] * (len(own) + 4),
        out_specs=[whole] * 2,
        out_shape=[jax.ShapeDtypeStruct((parts // 2, 2 * kd // parts, 128), jnp.float32)] * 2,
        scratch_shapes=[pltpu.VMEM((2, tokens // TB, rank, width), jnp.float32)],
        compiler_params=pltpu.CompilerParams(vmem_limit_bytes=VMEM),
        cost_estimate=pl.CostEstimate(
            flops=8 * tokens * width * rank, bytes_accessed=4 * tokens * width, transcendentals=0
        ),
        name="feature_shares",
    )(x, g, *own, other, bits)


def valid_kernel(rank, v_ref, hl_ref, sq_ref):
    v = v_ref[...]
    rows, cols = v.shape
    ks = cols // rank
    goes = lax.broadcasted_iota(jnp.int32, (cols, cols), 0)
    came = lax.broadcasted_iota(jnp.int32, (cols, cols), 1)
    move = jnp.where((came % rank) * ks + came // rank == goes, 1.0, 0.0).astype(jnp.bfloat16)
    hl_ref[...] = mm(move, halves(v), NT).astype(jnp.bfloat16)
    total = mm(jnp.ones((8, cols), jnp.bfloat16), halves(v * v), NT)
    sq_ref[...] = total[:, :rows] + total[:, rows:]


def valid_terms(v, rank):
    rows, cols = v.shape
    whole = pl.BlockSpec(memory_space=pltpu.VMEM)
    return pl.pallas_call(
        functools.partial(valid_kernel, rank),
        in_specs=[whole],
        out_specs=[whole, whole],
        out_shape=[
            jax.ShapeDtypeStruct((cols, 2 * rows), jnp.bfloat16),
            jax.ShapeDtypeStruct((8, rows), jnp.float32),
        ],
        compiler_params=pltpu.CompilerParams(vmem_limit_bytes=VMEM // 2),
        cost_estimate=pl.CostEstimate(
            flops=4 * rows * cols * cols, bytes_accessed=8 * rows * cols, transcendentals=0
        ),
        name="valid_terms",
    )(v)


def flip(step, z, y):
    if step == STEP_A:
        return z ^ 1, y
    if step == STEP_F:
        return z ^ 4, y
    if step == STEP_Y:
        return z, y ^ 1
    return (z + 2 * (z & 1) - 1) & 7, y


def flips(step):
    pairs = []
    for i in range(16):
        z, y = flip(step, i >> 1, i & 1)
        pairs.append((i, z * 2 + y))
    return pairs


def origin(place, index):
    z, y = index >> 1, index & 1
    for step in (3, 2, 1, 0):
        if place >> step & 1:
            z, y = flip(step, z, y)
    return z * 2 + y


def dot_kernel(rank, f_ref, hl0_ref, sq0_ref, hl1_ref, sq1_ref, out_ref, t_ref):
    parts = out_ref.shape[0]
    rows = sq0_ref.shape[1]
    each = 2 * rows // parts
    t_ref[...] = jnp.transpose(jnp.sum(f_ref[...], 0))
    f = jnp.concatenate([t_ref[pl.ds(r, 8, stride=rank), :] for r in range(rank)], 1)
    own_sq = jnp.broadcast_to(jnp.sum(f * f, 1, keepdims=True), (8, 128))
    lane = lax.broadcasted_iota(jnp.int32, (8, 128), 1)
    origins = [origin(n, lax.axis_index("grp")) for n in range(parts // 2)]
    f = halves(f)
    for half, (hl_ref, sq_ref) in enumerate(((hl0_ref, sq0_ref), (hl1_ref, sq1_ref))):
        prod = mm(f, hl_ref[...], NN)
        dots = prod[:8, :rows] + (prod[8:, :rows] + prod[:8, rows:]) + prod[8:, rows:]
        line = lax.broadcasted_iota(jnp.int32, dots.shape, 0)
        dots = jnp.where(line == 6, sq_ref[...], dots)
        for n, part in enumerate(origins):
            begin, turn = divmod(n * each, 128)
            tile = dots[:, begin * 128 : (begin + 1) * 128]
            if turn:
                tile = pltpu.roll(tile, 128 - turn, 1)
            out_ref[part ^ half] = jnp.where(lane < each, tile, own_sq)


def partial_dots(f, terms, rank):
    whole = pl.BlockSpec(memory_space=pltpu.VMEM)
    return pl.pallas_call(
        functools.partial(dot_kernel, rank),
        in_specs=[whole] * 5,
        out_specs=whole,
        out_shape=jax.ShapeDtypeStruct((2 * f.shape[0], 8, 128), jnp.float32),
        scratch_shapes=[pltpu.VMEM((128, f.shape[1]), jnp.float32)],
        compiler_params=pltpu.CompilerParams(vmem_limit_bytes=VMEM // 2),
        name="partial_dots",
    )(f, *terms)


def on_device(x, g, a, b, bits, valid):
    tp = lax.axis_size("tp")
    rank = b.shape[0]
    seqs = x.shape[0] // LEN
    each = 16 * valid.shape[0] // tp
    swap_core = [(i, i ^ 1) for i in range(tp)]
    swap_y = [(i, i ^ 8) for i in range(tp)]
    same_core = [list(range(c, tp, 2)) for c in range(2)]
    turn_x = [[(i, (i & 9) | (((i >> 1) + k & 3) << 1)) for i in range(tp)] for k in range(4)]

    def gather(step, rows):
        return rows, lax.ppermute(rows, "grp", flips(step))

    tie = lax.optimization_barrier

    def from_group(step, rows):
        return lax.ppermute(rows, "grp", flips(step))

    keep, send, x, g = rank_rows(x, g, jnp.transpose(a), b)
    send, near = tie((send, valid))
    far = from_group(STEP_B, near)
    mine = keep + lax.ppermute(send, "tp", swap_core)
    came = [lax.ppermute(mine[k], "tp", turn_x[k]) for k in (1, 2, 3)]
    near = jnp.concatenate([near, far], 0)
    far = from_group(STEP_F, near)
    mine = mine[0] + came[0] + came[1] + came[2]
    mine = mine + lax.ppermute(mine, "tp", swap_y)
    mine, near, far = tie((mine, near, far))
    near = jnp.concatenate([near, far], 0)
    own = [mine] + [lax.ppermute(mine, "tp", turn_x[k]) for k in (1, 2, 3)]
    far = from_group(STEP_A, near)
    own, near = tie((own, jnp.concatenate([near, far], 0)))
    far = from_group(STEP_Y, near)
    other = lax.ppermute(jnp.stack(own), "tp", swap_core)
    keep, send = feature_shares(x, g, own, other, (2 * bits - 1).astype(jnp.bfloat16), tp)
    send, near = tie((send, near))
    near = valid_terms(near, rank)
    came = lax.ppermute(send, "tp", swap_core)
    came, near = tie((came, near))
    shares = lax.all_to_all(keep + came, "tp", 0, 0, axis_index_groups=same_core, tiled=True)
    far = valid_terms(far, rank)
    dots = partial_dots(shares, [*near, *far], rank)
    dots = lax.all_to_all(dots, "tp", 0, 0, tiled=True)
    total = jnp.sum(dots, 0)
    train = math.sqrt(K) / jnp.sqrt(total[:seqs, each : 2 * each] + EPS)
    return total[:seqs, :each] * train / jnp.sqrt(total[6:7, :each] + EPS)


def solution(mesh):
    return jax.shard_map(
        on_device,
        mesh=mesh,
        in_specs=(
            P("grp", "tp"),
            P("grp", "tp"),
            P("tp", None),
            P(None, "tp"),
            P("tp", None),
            P("grp", "tp"),
        ),
        out_specs=P("grp", "tp"),
        check_vma=False,
    )
```
